768 devices in a mesh: span: 32 (over x, z_hi, core), chord: 24 (over y, z_lo).
Axes of the slice: x: 4, y: 8, z: 12 (z_hi: 4, z_lo: 3; z = z_hi * 3 + z_lo), core: 2. Of those that a mesh axis runs over, the one named last changes fastest.
Arguments:
- traces: float32 [2, 45, 589824], P(None, None, ('span', 'chord')), may hold values from -6 to 6
- source: float32 [2, 135, 196608], P(None, None, ('span', 'chord')), may hold values from -6 to 6
- scales: float32 [135, 6144], P(None, ('span', 'chord')), may hold values from 0.5 to 2
- inverse_local: float32 [2, 135, 135], replicated, may hold values from -0.375 to 0.375
- lift_map: float32 [2, 135, 270], replicated, may hold values from -0.25 to 0.25
- trace_map: float32 [2, 270, 135], replicated, may hold values from -0.375 to 0.375
- stabilizer: float32 [2, 270, 270], replicated, may hold values from -0.25 to 0.25
- elem_faces: int32 [6144, 6], P(('span', 'chord')), may hold values from 0 to 39, as said below
- send_faces: int32 [32, 24, 4, 4], P('span', 'chord'), may hold values from 0 to 23, as said below
- counts: int32 [32, 24], P('span', 'chord'), may hold values from 4 to 8, as said below
Outputs:
- interior_field: float32 [2, 135, 196608], P(None, None, ('span', 'chord'))
- residual: float32 [2, 45, 589824], P(None, None, ('span', 'chord'))
The draws below stay inside these ranges and needn't reach their ends.
Inputs may be any that keep to these rules, and one draw needn't show every extreme that they name: `elem_faces`: in a partition, entries of element slots 4 and later are below 24; every ghost number is referenced exactly once. `send_faces`: the 4 entries of one partition and direction are distinct. `counts`: some partition is full.
All inputs are finite; a program needn't handle non-finite values.
Results may differ from the reference program's by a relative error of at most 0.0003.
Values sent between devices are 32-bit elements; how exact they have to be, the bound alone decides.
No kernel may reach another device: no remote copies, remote signals or barrier semaphores. Data moves between devices by JAX's collectives and lax.ppermute only.
A program may use at most 32 MiB of HBM per device.

```python
import math
import jax
import jax.numpy as jnp
from jax import lax

FACE_DOF = 45
CELL_DOF = 135
ANG = 32
E_CAP = 8
E_EDGE = 4
G = 4
F_OWN = 24
E_TOT = 6144
F_TOT = 18432
N_SPAN = 32
N_CHORD = 24


def draw_elem_faces(key, part):
    key = jax.random.fold_in(key, 11)
    devices_all = E_TOT // E_CAP
    subkeys = jax.random.split(key, devices_all)

    def one_partition(subkey):
        first_key, second_key, third_key = jax.random.split(subkey, 3)
        extra = jax.random.permutation(first_key, F_OWN)[:E_CAP].astype(jnp.int32)
        owned = jnp.concatenate([jnp.arange(F_OWN, dtype=jnp.int32), extra])
        owned = jax.random.permutation(second_key, owned)
        ghosts = F_OWN + jnp.arange(4 * G, dtype=jnp.int32)
        edge_refs = jax.random.permutation(third_key, jnp.concatenate([ghosts, owned[:E_CAP]]))
        inner_refs = owned[E_CAP:]
        return jnp.concatenate([edge_refs, inner_refs]).reshape(E_CAP, 6)
    return jax.vmap(one_partition)(subkeys).reshape(E_TOT, 6).astype(jnp.int32)


def draw_send_faces(key, part):
    key = jax.random.fold_in(key, 23)
    subkeys = jax.random.split(key, N_SPAN * N_CHORD * 4)
    picks = jax.vmap(lambda subkey: jax.random.permutation(subkey, F_OWN)[:G])(subkeys)
    return picks.reshape(N_SPAN, N_CHORD, 4, G).astype(jnp.int32)


def draw_counts(key, part):
    key = jax.random.fold_in(key, 37)
    first_key, second_key = jax.random.split(key)
    values = jax.random.randint(first_key, (N_SPAN * N_CHORD,), E_EDGE, E_CAP + 1)
    place = jax.random.randint(second_key, (), 0, N_SPAN * N_CHORD)
    values = values.at[place].set(E_CAP)
    return values.reshape(N_SPAN, N_CHORD).astype(jnp.int32)


def levels(own_key, dims, pieces, smallest, largest):
    factor_of, own = 1.0, jax.random.fold_in(own_key, 6)
    for dim, blocks in pieces:
        heights = jnp.exp(jax.random.uniform(jax.random.fold_in(own, dim), (blocks,), jnp.float32, smallest / len(pieces), largest / len(pieces)))
        factor_of = factor_of * jnp.repeat(heights, dims[dim] // blocks).reshape([-1 if axis == dim else 1 for axis in range(len(dims))])
    return factor_of


def scatter_about(key, shape, spread, reach, pieces=(), held_as=jnp.bfloat16):
    loudness = levels(key, shape, pieces, -0.22, 0.18) if pieces else 1.0
    values = jax.random.normal(key, shape, jnp.float32) * spread * loudness
    return jnp.minimum(jnp.maximum(values, -reach), reach).astype(held_as)


def setup_inputs(seed: int = 0) -> dict:
    streams_of = jax.random.split(jax.random.key(seed), 11)
    return {
        "traces": scatter_about(streams_of[0], (2, FACE_DOF, F_TOT * ANG), 1.0, 6.0, ((2, 768),), jnp.float32),
        "source": scatter_about(streams_of[1], (2, CELL_DOF, E_TOT * ANG), 1.0, 6.0, ((2, 768),), jnp.float32),
        "scales": jnp.clip(jnp.exp(math.log(2.0) - 1.3862944 * jax.random.uniform(streams_of[2], (CELL_DOF, E_TOT), jnp.float32) ** levels(streams_of[2], (CELL_DOF, E_TOT), ((1, 768),), -0.2, 0.2)), 0.5, 2.0),
        "inverse_local": scatter_about(streams_of[3], (2, CELL_DOF, CELL_DOF), (2 * CELL_DOF) ** -0.5, 0.375, (), jnp.float32),
        "lift_map": scatter_about(streams_of[4], (2, CELL_DOF, 6 * FACE_DOF), (12 * FACE_DOF) ** -0.5, 0.25, (), jnp.float32),
        "trace_map": scatter_about(streams_of[5], (2, 6 * FACE_DOF, CELL_DOF), (2 * CELL_DOF) ** -0.5, 0.375, (), jnp.float32),
        "stabilizer": scatter_about(streams_of[6], (2, 6 * FACE_DOF, 6 * FACE_DOF), (12 * FACE_DOF) ** -0.5, 0.25, (), jnp.float32),
        "elem_faces": draw_elem_faces(jax.random.fold_in(streams_of[10], 71), 0),
        "send_faces": draw_send_faces(jax.random.fold_in(streams_of[10], 71), 0),
        "counts": draw_counts(jax.random.fold_in(streams_of[10], 71), 0),
    }


def exact_dot(left, right):
    return jnp.dot(left, right, precision=lax.Precision.HIGHEST, preferred_element_type=jnp.float32)


def complex_block(matrix):
    real_part = matrix[0]
    imag_part = matrix[1]
    top = jnp.concatenate([real_part, -imag_part], axis=1)
    bottom = jnp.concatenate([imag_part, real_part], axis=1)
    return jnp.concatenate([top, bottom], axis=0)


def reference(traces, source, scales, inverse_local, lift_map, trace_map, stabilizer, elem_faces, send_faces, counts):
    devices_all = N_SPAN * N_CHORD
    phases = 2.0 * math.pi * jnp.arange(ANG).astype(jnp.float32) / ANG
    face_table = traces.reshape(2, FACE_DOF, F_TOT, ANG)
    send_lists = send_faces.reshape(devices_all, 4, G)
    faces_all = elem_faces.reshape(devices_all, E_CAP, 6)
    counts_flat = counts.reshape(devices_all)
    block_inv = complex_block(inverse_local)
    block_lift = complex_block(lift_map)
    block_trace = complex_block(trace_map)
    block_stab = complex_block(stabilizer)

    def advance(totals, device_id):
        span_id = device_id // N_CHORD
        chord_id = device_id % N_CHORD
        lower_id = span_id * N_CHORD + jnp.maximum(chord_id - 1, 0)
        upper_id = span_id * N_CHORD + jnp.minimum(chord_id + 1, N_CHORD - 1)
        before_id = ((span_id - 1) % N_SPAN) * N_CHORD + chord_id
        after_id = ((span_id + 1) % N_SPAN) * N_CHORD + chord_id
        neighbours = jnp.stack([lower_id, upper_id, before_id, after_id]).astype(jnp.int32)
        chosen = jnp.stack([send_lists[lower_id, 1], send_lists[upper_id, 0],
                            send_lists[before_id, 3], send_lists[after_id, 2]])
        ghost_global = (chosen + neighbours[:, None] * F_OWN).reshape(-1).astype(jnp.int32)
        valid_side = jnp.stack([jnp.where(chord_id > 0, 1.0, 0.0), jnp.where(chord_id < N_CHORD - 1, 1.0, 0.0),
                                jnp.ones((), jnp.float32), jnp.ones((), jnp.float32)]).astype(jnp.float32)
        sign_side = jnp.stack([jnp.zeros((), jnp.float32), jnp.zeros((), jnp.float32),
                               jnp.where(span_id == 0, -1.0, 0.0), jnp.where(span_id == N_SPAN - 1, 1.0, 0.0)]).astype(jnp.float32)
        local = faces_all[device_id]
        is_own = local < F_OWN
        ghost_pos = jnp.clip(local - F_OWN, 0, 4 * G - 1).astype(jnp.int32)
        global_face = jnp.where(is_own, device_id * F_OWN + local, ghost_global[ghost_pos]).astype(jnp.int32)
        validity = jnp.where(is_own, 1.0, valid_side[ghost_pos // G]).astype(jnp.float32).T
        signs = jnp.where(is_own, 0.0, sign_side[ghost_pos // G]).astype(jnp.float32).T
        face_index = global_face.T
        gathered = face_table[:, :, face_index, :]
        cosine = jnp.cos(signs[:, :, None] * phases)
        sine_part = jnp.sin(signs[:, :, None] * phases)
        weight = validity[:, :, None]
        real_part = (gathered[0] * cosine - gathered[1] * sine_part) * weight
        imag_part = (gathered[0] * sine_part + gathered[1] * cosine) * weight
        element_trace = jnp.stack([real_part, imag_part])
        trace_cols = jnp.transpose(element_trace, (0, 2, 1, 3, 4)).reshape(12 * FACE_DOF, E_CAP * ANG)
        source_cols = lax.dynamic_slice_in_dim(source, device_id * E_CAP * ANG, E_CAP * ANG, 2).reshape(2 * CELL_DOF, E_CAP * ANG)
        scale_cols = lax.dynamic_slice_in_dim(scales, device_id * E_CAP, E_CAP, 1)
        live_mask = (jnp.arange(E_CAP) < counts_flat[device_id]).astype(jnp.float32)
        interior_rhs = source_cols - exact_dot(block_lift, trace_cols)
        interior_rhs = (interior_rhs.reshape(2, CELL_DOF, E_CAP, ANG) * scale_cols[None, :, :, None]).reshape(2 * CELL_DOF, E_CAP * ANG)
        interior = exact_dot(block_inv, interior_rhs).reshape(2, CELL_DOF, E_CAP, ANG) * live_mask[None, None, :, None]
        face_terms = exact_dot(block_trace, interior.reshape(2 * CELL_DOF, E_CAP * ANG)) + exact_dot(block_stab, trace_cols)
        face_terms = face_terms.reshape(2, 6, FACE_DOF, E_CAP, ANG) * live_mask[None, None, None, :, None]
        face_terms = jnp.transpose(face_terms, (0, 2, 1, 3, 4))
        back_real = (face_terms[0] * cosine + face_terms[1] * sine_part) * weight
        back_imag = (face_terms[1] * cosine - face_terms[0] * sine_part) * weight
        totals = totals.at[:, :, face_index, :].add(jnp.stack([back_real, back_imag]))
        return totals, interior.reshape(2, CELL_DOF, E_CAP * ANG)

    start = jnp.zeros((2, FACE_DOF, F_TOT, ANG), jnp.float32)
    totals, interiors = lax.scan(advance, start, jnp.arange(devices_all, dtype=jnp.int32))
    interior_field = jnp.transpose(interiors, (1, 2, 0, 3)).reshape(2, CELL_DOF, E_TOT * ANG)
    residual = totals.reshape(2, FACE_DOF, F_TOT * ANG)
    return interior_field, residual
```

```python
import math

import jax
import jax.numpy as jnp
from jax import lax
from jax.experimental import pallas as pl
from jax.experimental.pallas import tpu as pltpu
from jax.sharding import PartitionSpec as P

ANG = 32
FD = 45
CD = 135
TILE = 128
F32 = jnp.float32
BF16 = jnp.bfloat16

VM = pl.BlockSpec(memory_space=pltpu.VMEM)
SM = pl.BlockSpec(memory_space=pltpu.SMEM)
HB = pl.BlockSpec(memory_space=pltpu.HBM)


def place():
    s, c = lax.axis_index("span"), lax.axis_index("chord")
    return s, c, lax.axis_size("span")


def sides(s, c):
    odd_s, odd_c = s & 1, c & 1
    return 3 - odd_s, 2 + odd_s, 1 - odd_c, odd_c


def lane_group(rows):
    return lax.broadcasted_iota(jnp.int32, (rows, TILE), 1) >> 5


def shifted(block, source, target):
    return pltpu.roll(block, ((target - source) & 3) * ANG, 1)


def split(x):
    high = x.astype(BF16)
    return high, (x - high.astype(F32)).astype(BF16)


def mm(left, right):
    return jnp.dot(left, right, preferred_element_type=F32)


def triple(left, right):
    (lh, ll), (rh, rl) = left, right
    return mm(lh, rh) + (mm(lh, rl) + mm(ll, rh))


def complex_parts(real_rows, imag_rows):
    re = real_rows[:, :TILE] - imag_rows[:, TILE:]
    im = imag_rows[:, :TILE] + real_rows[:, TILE:]
    return re, im


def rows_of(ref, tile, part, tiles, count):
    return ref.reshape(count * tiles * 2, TILE), pl.ds(2 * tile + part, count, stride=2 * tiles)


def element_columns(first, faces, read, cols, src, scales, alive, ops, field, terms):
    half = first // 4
    group = lane_group(FD)
    for m in range(6):
        refs = [faces[first + k, m] for k in range(4)]
        for part in range(2):
            value = None
            for k, ref in enumerate(refs):
                moved = shifted(read(ref >> 2, part), ref & 3, k)
                value = moved if k == 0 else jnp.where(group == k, moved, value)
            cols[pl.ds(FD * m, FD), pl.ds(TILE * part, TILE)] = value
    x = split(cols[...])
    lh, ll, ih, il, th, tl, sh, sl = ops
    re, im = complex_parts(*[triple((lh[p], ll[p]), x) for p in range(2)])
    scale = scales[:, pl.ds(TILE * half, TILE)]
    rhs = split(jnp.concatenate([scale * (src[0, half] - re), scale * (src[1, half] - im)], axis=1))
    re, im = complex_parts(*[triple((ih[p], il[p]), rhs) for p in range(2)])
    alive = alive[:, pl.ds(TILE * half, TILE)]
    re, im = re * alive, im * alive
    field[0], field[1] = re, im
    inner = split(jnp.concatenate([re, im], axis=1))
    out = [triple((th[p], tl[p]), inner) + triple((sh[p], sl[p]), x) for p in range(2)]
    for part, value in enumerate(complex_parts(*out)):
        value = value * alive
        for m in range(6):
            terms[m, part] = value[FD * m : FD * m + FD]


def turn(re, im, sign, angles):
    cosine = jnp.where(sign == 0, 1.0, angles[0:1, :])
    sine = sign.astype(F32) * angles[1:2, :]
    return re * cosine - im * sine, re * sine + im * cosine


def pack_kernel(send_far, traces, on_chip, span, even, odd, near, send_near, send, sems):
    s, c, _ = place()
    group = lane_group(FD)
    numbers = pltpu.make_async_copy(send_far, send, sems.at[0])
    values = pltpu.make_async_copy(traces, near, sems.at[1])
    keep = pltpu.make_async_copy(send_far, send_near, sems.at[2])
    numbers.start()
    values.start()
    keep.start()
    numbers.wait()
    values.wait()
    keep.wait()
    for side, out in zip(sides(s, c), (on_chip, span, even, odd)):
        faces = [send[0, 0, side, j] for j in range(4)]
        for part in range(2):
            value = None
            for j, face in enumerate(faces):
                flat, rows = rows_of(near, face >> 2, part, 6, FD)
                moved = shifted(flat[rows, :], face & 3, j)
                value = moved if j == 0 else jnp.where(group == j, moved, value)
            out[part] = value


def prepare_kernel(lift, inv, trace, stab, source, numbers, total, scales, *rest):
    outs, (src, wide, angles, faces, alive) = rest[:8], rest[8:13]
    held, plain, sems = rest[13:18], rest[18], rest[19]
    copies = [
        pltpu.make_async_copy(ref, slot, sems.at[k])
        for k, (ref, slot) in enumerate(zip((lift, inv, trace, stab, source), held))
    ]
    copies.append(pltpu.make_async_copy(numbers, faces, sems.at[5]))
    for copy in copies:
        copy.start()
    turns = lax.broadcasted_iota(jnp.int32, (1, TILE), 1) & (ANG - 1)
    sigma = 2.0 * math.pi * turns.astype(F32) / ANG
    angles[0:1, :], angles[1:2, :] = jnp.cos(sigma), jnp.sin(sigma)
    column = lax.broadcasted_iota(jnp.int32, (CD, 2 * TILE), 1) >> 5
    tall = scales[...].T
    value = None
    for e in range(8):
        spread = jnp.broadcast_to(tall[:, e : e + 1], (CD, 2 * TILE))
        value = spread if e == 0 else jnp.where(column == e, spread, value)
    wide[...] = value
    for k, (copy, slot) in enumerate(zip(copies[:4], held)):
        copy.wait()
        for part in range(2):
            rows, _, columns = slot.shape
            plain[pl.ds(0, rows), pl.ds(0, columns)] = slot[:, part, :]
            matrix = plain[pl.ds(0, rows), pl.ds(0, columns)]
            if k == 2:
                matrix = matrix.T
            outs[2 * k][part], outs[2 * k + 1][part] = split(matrix)
    copies[4].wait()
    for part in range(2):
        for half in range(2):
            flat, rows = rows_of(held[4], half, part, 2, CD)
            src[part, half] = flat[rows, :]
    copies[5].wait()
    element = lax.broadcasted_iota(jnp.int32, (1, 2 * TILE), 1) >> 5
    alive[...] = (element < total[...]).astype(F32)


def edge_kernel(faces, traces, span, odd, even, on_chip, src, scales, alive, angles, *rest):
    ops, (b_on, b_span, b_even, b_odd, field, terms, table, cols, where) = rest[:8], rest[8:]
    s, c, length = place()
    side = sides(s, c)
    sign = jnp.where(s == 0, -1, jnp.where(s == length - 1, 1, 0))
    for tile in range(6):
        for part in range(2):
            flat, rows = rows_of(traces, tile, part, 6, FD)
            table[tile, part] = flat[rows, :]
    for d, ref in zip((side[0], side[2], side[3]), (on_chip, even, odd)):
        for part in range(2):
            table[6 + d, part] = ref[part]
    table[6 + side[1], 0], table[6 + side[1], 1] = turn(span[0], span[1], sign, angles)
    for k in range(4):
        for m in range(6):
            where[faces[k, m]] = 4 * m + k
    element_columns(
        0, faces, lambda tile, part: table[tile, part], cols, src, scales, alive, ops, field, terms
    )
    group = lane_group(FD)
    for d, ref in zip(side, (b_on, b_span, b_even, b_odd)):
        spots = [where[24 + 4 * d + j] for j in range(4)]
        parts = []
        for part in range(2):
            value = None
            for j, spot in enumerate(spots):
                moved = shifted(terms[spot >> 2, part], spot & 3, j)
                value = moved if j == 0 else jnp.where(group == j, moved, value)
            parts.append(value)
        if ref is b_span:
            parts = turn(*parts, -sign, angles)
        ref[0], ref[1] = parts


def inner_kernel(faces, traces, src, scales, alive, edge_field, edge_terms, *rest):
    ops, (field, sums, cols, inner, terms) = rest[:8], rest[8:]

    def read(tile, part):
        flat, rows = rows_of(traces, tile, part, 6, FD)
        return flat[rows, :]

    element_columns(4, faces, read, cols, src, scales, alive, ops, inner, terms)
    for part in range(2):
        for half, values in enumerate((edge_field, inner)):
            flat, rows = rows_of(field, half, part, 2, CD)
            flat[rows, :] = values[part]
    sums[...] = jnp.zeros(sums.shape, F32)
    group = lane_group(FD)
    for source, first in ((edge_terms, 0), (terms, 4)):
        for m in range(6):
            for k in range(4):
                ref = faces[first + k, m]
                hit = group == (ref & 3)
                for part in range(2):
                    sums[ref >> 2, part] += jnp.where(hit, shifted(source[m, part], k, ref & 3), 0.0)


def final_kernel(send, total, span, even, odd, on_chip, out, sums):
    s, c, _ = place()
    sums[...] = total[pl.ds(0, 6)]
    group = lane_group(FD)
    for side, ref in zip(sides(s, c), (on_chip, span, even, odd)):
        for j in range(4):
            face = send[0, 0, side, j]
            hit = group == (face & 3)
            for part in range(2):
                sums[face >> 2, part] += jnp.where(hit, shifted(ref[part], j, face & 3), 0.0)
    for tile in range(6):
        for part in range(2):
            flat, rows = rows_of(out, tile, part, 6, FD)
            flat[rows, :] = sums[tile, part]


def swaps(count, periodic):
    even = [(i, i ^ 1) for i in range(count)]
    odd = [pair for i in range(1, count - 1, 2) for pair in ((i, i + 1), (i + 1, i))]
    if periodic:
        odd += [(count - 1, 0), (0, count - 1)]
    return even, odd


def exchange(on_chip, span, even, odd, odd_first):
    span_even, span_odd = swaps(lax.axis_size("span"), True)
    chord_even, chord_odd = swaps(lax.axis_size("chord"), False)
    plan = [(even, "chord", chord_even), (odd, "chord", chord_odd)]
    if odd_first:
        plan.reverse()
    plan = [(span, "span", span_odd), *plan, (on_chip, "span", span_even)]
    return [lax.ppermute(*step) for step in plan]


def shape(*dims, dtype=F32):
    return jax.ShapeDtypeStruct(dims, dtype)


def params(**kwargs):
    return pltpu.CompilerParams(vmem_limit_bytes=32 * 1024 * 1024, **kwargs)


def cost(flops, size):
    return pl.CostEstimate(flops=flops, bytes_accessed=size, transcendentals=0)


def interleaved(array):
    _, rows, lanes = array.shape
    return array.transpose(1, 0, 2).reshape(rows, 2, lanes // TILE, TILE).transpose(0, 2, 1, 3)


def hbm(array):
    return pltpu.with_memory_space_constraint(array, pltpu.HBM)


def parted(array):
    rows, tiles = array.shape[:2]
    return array.transpose(0, 2, 1, 3).reshape(rows, 2, tiles * TILE).transpose(1, 0, 2)


def local(
    traces, source, scales, inverse_local, lift_map, trace_map, stabilizer, elem_faces, send_faces, counts
):
    buffers = (shape(2, FD, TILE),) * 4
    linear = shape(FD, 6, 2, TILE)

    *sent, near, send_near = pl.pallas_call(
        pack_kernel,
        out_shape=buffers + (linear, shape(*send_faces.shape, dtype=jnp.int32)),
        in_specs=[HB, HB],
        out_specs=[VM] * 6,
        scratch_shapes=[pltpu.SMEM((1, 1, 4, 4), jnp.int32), pltpu.SemaphoreType.DMA((3,))],
        compiler_params=params(),
        cost_estimate=cost(0, 600_000),
        name="pack",
    )(hbm(send_faces), hbm(interleaved(traces)))
    ghosts = exchange(*sent, True)
    weights = (
        lift_map.transpose(1, 0, 2),
        inverse_local.transpose(1, 0, 2),
        trace_map.transpose(2, 0, 1),
        stabilizer.transpose(1, 0, 2),
    )
    wide_source = interleaved(source)
    *ops, src, wide, angles, faces, alive = pl.pallas_call(
        prepare_kernel,
        out_shape=[
            shape(*w.shape, dtype=BF16)
            for w in (lift_map, inverse_local, trace_map, stabilizer)
            for _ in range(2)
        ]
        + [shape(2, 2, CD, TILE), shape(CD, 2 * TILE), shape(2, TILE)]
        + [shape(*elem_faces.shape, dtype=jnp.int32), shape(1, 2 * TILE)],
        in_specs=[HB] * 6 + [VM] * 2,
        out_specs=[VM] * 13,
        scratch_shapes=[pltpu.VMEM(w.shape, F32) for w in weights + (wide_source,)]
        + [
            pltpu.VMEM(weights[3].shape[::2], F32),
            pltpu.SemaphoreType.DMA((6,)),
        ],
        compiler_params=params(),
        cost_estimate=cost(0, 3_000_000),
        name="prepare",
    )(*map(hbm, weights), hbm(wide_source), hbm(elem_faces), counts, scales.T)
    *back, edge_field, edge_terms = pl.pallas_call(
        edge_kernel,
        out_shape=buffers + (shape(2, CD, TILE), shape(6, 2, FD, TILE)),
        in_specs=[SM] + [VM] * 17,
        out_specs=[VM] * 6,
        scratch_shapes=[
            pltpu.VMEM((10, 2, FD, TILE), F32),
            pltpu.VMEM((6 * FD, 2 * TILE), F32),
            pltpu.SMEM((40,), jnp.int32),
        ],
        compiler_params=params(),
        cost_estimate=cost(1_000_000_000, 3_000_000),
        name="edge_elements",
    )(faces, near, *ghosts, src, wide, alive, angles, *ops)
    returned = exchange(*back, False)
    field, total = pl.pallas_call(
        inner_kernel,
        out_shape=(shape(CD, 2, 2, TILE), shape(10, 2, FD, TILE)),
        in_specs=[SM] + [VM] * 14,
        out_specs=[VM] * 2,
        scratch_shapes=[
            pltpu.VMEM((6 * FD, 2 * TILE), F32),
            pltpu.VMEM((2, CD, TILE), F32),
            pltpu.VMEM((6, 2, FD, TILE), F32),
        ],
        compiler_params=params(),
        cost_estimate=cost(1_000_000_000, 3_000_000),
        name="inner_elements",
    )(faces, near, src, wide, alive, edge_field, edge_terms, *ops)
    residual = pl.pallas_call(
        final_kernel,
        out_shape=linear,
        in_specs=[SM] + [VM] * 5,
        out_specs=VM,
        scratch_shapes=[pltpu.VMEM((6, 2, FD, TILE), F32)],
        compiler_params=params(),
        cost_estimate=cost(0, 1_000_000),
        name="final_sum",
    )(send_near, total, *returned)
    return parted(field), parted(residual)


def solution(mesh):
    spread = ("span", "chord")
    in_specs = (
        P(None, None, spread),
        P(None, None, spread),
        P(None, spread),
        P(),
        P(),
        P(),
        P(),
        P(spread, None),
        P("span", "chord", None, None),
        P("span", "chord"),
    )
    out_specs = (P(None, None, spread), P(None, None, spread))
    return jax.shard_map(local, mesh=mesh, in_specs=in_specs, out_specs=out_specs, check_vma=False)
```

```python
import math

import jax
import jax.numpy as jnp
from jax import lax
from jax.experimental import pallas as pl
from jax.experimental.pallas import tpu as pltpu
from jax.sharding import PartitionSpec as P

ANG = 32
EARLY = 0
FD = 45
CD = 135
TILE = 128
F32 = jnp.float32
BF16 = jnp.bfloat16

VM = pl.BlockSpec(memory_space=pltpu.VMEM)
SM = pl.BlockSpec(memory_space=pltpu.SMEM)
HB = pl.BlockSpec(memory_space=pltpu.HBM)


def place():
    s, c = lax.axis_index("span"), lax.axis_index("chord")
    return s, c, lax.axis_size("span")


def sides(s, c):
    odd_s, odd_c = s & 1, c & 1
    return 3 - odd_s, 2 + odd_s, 1 - odd_c, odd_c


def lane_group(rows):
    return lax.broadcasted_iota(jnp.int32, (rows, TILE), 1) >> 5


def shifted(block, source, target):
    return pltpu.roll(block, ((target - source) & 3) * ANG, 1)


def split(x):
    high = x.astype(BF16)
    return high, (x - high.astype(F32)).astype(BF16)


def mm(left, right):
    return jnp.dot(left, right, preferred_element_type=F32)


def triple(left, right):
    (lh, ll), (rh, rl) = left, right
    return mm(lh, rh) + (mm(lh, rl) + mm(ll, rh))


def complex_parts(real_rows, imag_rows):
    re = real_rows[:, :TILE] - imag_rows[:, TILE:]
    im = imag_rows[:, :TILE] + real_rows[:, TILE:]
    return re, im


def rows_of(ref, tile, part, tiles, count):
    return ref.reshape(count * tiles * 2, TILE), pl.ds(2 * tile + part, count, stride=2 * tiles)


def element_columns(first, faces, read, cols, src, scales, alive, ops, field, terms):
    half = first // 4
    group = lane_group(FD)
    for m in range(6):
        refs = [faces[first + k, m] for k in range(4)]
        for part in range(2):
            value = None
            for k, ref in enumerate(refs):
                moved = shifted(read(ref >> 2, part), ref & 3, k)
                value = moved if k == 0 else jnp.where(group == k, moved, value)
            cols[pl.ds(FD * m, FD), pl.ds(TILE * part, TILE)] = value
    x = split(cols[...])
    lh, ll, ih, il, th, tl, sh, sl = ops
    re, im = complex_parts(*[triple((lh[p], ll[p]), x) for p in range(2)])
    scale = scales[:, pl.ds(TILE * half, TILE)]
    rhs = split(jnp.concatenate([scale * (src[0, half] - re), scale * (src[1, half] - im)], axis=1))
    re, im = complex_parts(*[triple((ih[p], il[p]), rhs) for p in range(2)])
    alive = 1.0 if alive is None else alive[:, pl.ds(TILE * half, TILE)]
    re, im = re * alive, im * alive
    field[0], field[1] = re, im
    inner = split(jnp.concatenate([re, im], axis=1))
    out = [triple((th[p], tl[p]), inner) + triple((sh[p], sl[p]), x) for p in range(2)]
    for part, value in enumerate(complex_parts(*out)):
        value = value * alive
        for m in range(6):
            terms[m, part] = value[FD * m : FD * m + FD]


def turn(re, im, sign, angles):
    cosine = jnp.where(sign == 0, 1.0, angles[0:1, :])
    sine = sign.astype(F32) * angles[1:2, :]
    return re * cosine - im * sine, re * sine + im * cosine


def early(s):
    return ((s >> 1) & 3) <= EARLY


def pack_kernel(send_far, traces, faces_far, *rest):
    weights, (on_chip, span, even, odd, near, send_near, faces_near) = rest[:6], rest[6:13]
    ops, (src, wide, angles, field, terms) = rest[13:21], rest[21:26]
    held, (cols, plain, sems) = rest[26:32], rest[32:]
    s, c, _ = place()
    group = lane_group(FD)
    pairs = ((send_far, send_near), (traces, near), (faces_far, faces_near))
    pairs += tuple(zip(weights, held))
    copies = [pltpu.make_async_copy(a, b, sems.at[k]) for k, (a, b) in enumerate(pairs)]
    for copy in copies:
        copy.start()
    for copy in copies[:2]:
        copy.wait()

    def read(tile, part):
        flat, rows = rows_of(near, tile, part, 6, FD)
        return flat[rows, :]

    for side, out in zip(sides(s, c), (on_chip, span, even, odd)):
        numbers = [send_near[0, 0, side, j] for j in range(4)]
        for part in range(2):
            value = None
            for j, face in enumerate(numbers):
                moved = shifted(read(face >> 2, part), face & 3, j)
                value = moved if j == 0 else jnp.where(group == j, moved, value)
            out[part] = value
    for copy in copies[2:]:
        copy.wait()

    @pl.when(early(s))
    def _():
        prepare(held, ops, src, wide, angles, plain)
        element_columns(4, faces_near, read, cols, src, wide, None, ops, field, terms)


def prepare(held, ops, src, wide, angles, plain):
    turns = lax.broadcasted_iota(jnp.int32, (1, TILE), 1) & (ANG - 1)
    sigma = 2.0 * math.pi * turns.astype(F32) / ANG
    angles[0:1, :], angles[1:2, :] = jnp.cos(sigma), jnp.sin(sigma)
    for k, slot in enumerate(held[:4]):
        for part in range(2):
            rows, _, columns = slot.shape
            plain[pl.ds(0, rows), pl.ds(0, columns)] = slot[:, part, :]
            matrix = plain[pl.ds(0, rows), pl.ds(0, columns)]
            if k == 2:
                matrix = matrix.T
            ops[2 * k][part], ops[2 * k + 1][part] = split(matrix)
    for part in range(2):
        for half in range(2):
            flat, rows = rows_of(held[4], half, part, 2, CD)
            src[part, half] = flat[rows, :]
    column = lax.broadcasted_iota(jnp.int32, (CD, 2 * TILE), 1) >> 5
    tall = held[5][...].T
    value = None
    for e in range(8):
        spread = jnp.broadcast_to(tall[:, e : e + 1], (CD, 2 * TILE))
        value = spread if e == 0 else jnp.where(column == e, spread, value)
    wide[...] = value


def prepare_kernel(*refs):
    held, outs, plain = refs[:6], refs[17:28], refs[28]

    @pl.when(jnp.logical_not(early(place()[0])))
    def _():
        prepare(held, outs[:8], *outs[8:], plain)


def edge_kernel(faces, traces, span, odd, even, on_chip, src, scales, alive, angles, *rest):
    ops, (b_on, b_span, b_even, b_odd, field, terms, table, cols, where) = rest[:8], rest[8:]
    s, c, length = place()
    side = sides(s, c)
    sign = jnp.where(s == 0, -1, jnp.where(s == length - 1, 1, 0))
    for tile in range(6):
        for part in range(2):
            flat, rows = rows_of(traces, tile, part, 6, FD)
            table[tile, part] = flat[rows, :]
    for d, ref in zip((side[0], side[2], side[3]), (on_chip, even, odd)):
        for part in range(2):
            table[6 + d, part] = ref[part]
    table[6 + side[1], 0], table[6 + side[1], 1] = turn(span[0], span[1], sign, angles)
    for k in range(4):
        for m in range(6):
            where[faces[k, m]] = 4 * m + k
    element_columns(
        0, faces, lambda tile, part: table[tile, part], cols, src, scales, alive, ops, field, terms
    )
    group = lane_group(FD)
    for d, ref in zip(side, (b_on, b_span, b_even, b_odd)):
        spots = [where[24 + 4 * d + j] for j in range(4)]
        parts = []
        for part in range(2):
            value = None
            for j, spot in enumerate(spots):
                moved = shifted(terms[spot >> 2, part], spot & 3, j)
                value = moved if j == 0 else jnp.where(group == j, moved, value)
            parts.append(value)
        if ref is b_span:
            parts = turn(*parts, -sign, angles)
        ref[0], ref[1] = parts


def inner_kernel(faces, traces, src, scales, alive, edge_field, edge_terms, ahead_field, ahead_terms, *rest):
    ops, (field, sums, cols, inner, terms) = rest[:8], rest[8:]
    ahead = early(place()[0])

    def read(tile, part):
        flat, rows = rows_of(traces, tile, part, 6, FD)
        return flat[rows, :]

    @pl.when(ahead)
    def _():
        inner[...] = ahead_field[...]
        terms[...] = ahead_terms[...]

    @pl.when(jnp.logical_not(ahead))
    def _():
        element_columns(4, faces, read, cols, src, scales, None, ops, inner, terms)

    live = alive[:, pl.ds(TILE, TILE)]
    for part in range(2):
        inner[part] *= live
        for m in range(6):
            terms[m, part] *= live
        for half, values in enumerate((edge_field, inner)):
            flat, rows = rows_of(field, half, part, 2, CD)
            flat[rows, :] = values[part]
    sums[...] = jnp.zeros(sums.shape, F32)
    group = lane_group(FD)
    for source, first in ((edge_terms, 0), (terms, 4)):
        for m in range(6):
            for k in range(4):
                ref = faces[first + k, m]
                hit = group == (ref & 3)
                for part in range(2):
                    sums[ref >> 2, part] += jnp.where(hit, shifted(source[m, part], k, ref & 3), 0.0)


def final_kernel(send, total, span, even, odd, on_chip, out, sums):
    s, c, _ = place()
    sums[...] = total[pl.ds(0, 6)]
    group = lane_group(FD)
    for side, ref in zip(sides(s, c), (on_chip, span, even, odd)):
        for j in range(4):
            face = send[0, 0, side, j]
            hit = group == (face & 3)
            for part in range(2):
                sums[face >> 2, part] += jnp.where(hit, shifted(ref[part], j, face & 3), 0.0)
    for tile in range(6):
        for part in range(2):
            flat, rows = rows_of(out, tile, part, 6, FD)
            flat[rows, :] = sums[tile, part]


def swaps(count, periodic):
    even = [(i, i ^ 1) for i in range(count)]
    odd = [pair for i in range(1, count - 1, 2) for pair in ((i, i + 1), (i + 1, i))]
    if periodic:
        odd += [(count - 1, 0), (0, count - 1)]
    return even, odd


def exchange(on_chip, span, even, odd, odd_first):
    span_even, span_odd = swaps(lax.axis_size("span"), True)
    chord_even, chord_odd = swaps(lax.axis_size("chord"), False)
    plan = [(even, "chord", chord_even), (odd, "chord", chord_odd)]
    if odd_first:
        plan.reverse()
    plan = [(span, "span", span_odd), *plan, (on_chip, "span", span_even)]
    return [lax.ppermute(*step) for step in plan]


def shape(*dims, dtype=F32):
    return jax.ShapeDtypeStruct(dims, dtype)


def params(**kwargs):
    return pltpu.CompilerParams(vmem_limit_bytes=32 * 1024 * 1024, **kwargs)


def cost(flops, size):
    return pl.CostEstimate(flops=flops, bytes_accessed=size, transcendentals=0)


def interleaved(array):
    _, rows, lanes = array.shape
    return array.transpose(1, 0, 2).reshape(rows, 2, lanes // TILE, TILE).transpose(0, 2, 1, 3)


def hbm(array):
    return pltpu.with_memory_space_constraint(array, pltpu.HBM)


def parted(array):
    rows, tiles = array.shape[:2]
    return array.transpose(0, 2, 1, 3).reshape(rows, 2, tiles * TILE).transpose(1, 0, 2)


def local(
    traces, source, scales, inverse_local, lift_map, trace_map, stabilizer, elem_faces, send_faces, counts
):
    buffers = (shape(2, FD, TILE),) * 4
    linear = shape(FD, 6, 2, TILE)

    weights = (
        lift_map.transpose(1, 0, 2),
        inverse_local.transpose(1, 0, 2),
        trace_map.transpose(2, 0, 1),
        stabilizer.transpose(1, 0, 2),
        interleaved(source),
        scales.T,
    )
    weights = tuple(map(hbm, weights))
    prepared = [
        shape(*w.shape, dtype=BF16)
        for w in (lift_map, inverse_local, trace_map, stabilizer)
        for _ in range(2)
    ] + [shape(2, 2, CD, TILE), shape(CD, 2 * TILE), shape(2, TILE)]
    held = [shape(*w.shape) for w in weights]
    plain = pltpu.VMEM(weights[3].shape[::2], F32)
    results = [shape(2, CD, TILE), shape(6, 2, FD, TILE)]
    numbers = [pltpu.SMEM(a.shape, jnp.int32) for a in (send_faces, elem_faces)]
    *packed, ahead_field, ahead_terms, k0, k1, k2, k3, k4, k5 = pl.pallas_call(
        pack_kernel,
        out_shape=[*buffers, linear, *numbers, *prepared, *results, *held],
        in_specs=[HB] * 9,
        out_specs=[VM] * 5 + [SM] * 2 + [VM] * 19,
        scratch_shapes=[
            pltpu.VMEM((6 * FD, 2 * TILE), F32),
            plain,
            pltpu.SemaphoreType.DMA((9,)),
        ],
        compiler_params=params(),
        cost_estimate=cost(0, 600_000),
        name="pack",
    )(hbm(send_faces), hbm(interleaved(traces)), hbm(elem_faces), *weights)
    sent, near, send_near, faces, ready = packed[:4], packed[4], packed[5], packed[6], packed[7:]
    ghosts = exchange(*sent, True)
    ready = pl.pallas_call(
        prepare_kernel,
        out_shape=prepared,
        in_specs=[VM] * 17,
        out_specs=[VM] * 11,
        input_output_aliases={6 + k: k for k in range(11)},
        scratch_shapes=[plain],
        compiler_params=params(),
        cost_estimate=cost(0, 3_000_000),
        name="prepare",
    )(k0, k1, k2, k3, k4, k5, *ready)
    ops, (src, wide, angles) = ready[:8], ready[8:]
    alive = ((jnp.arange(2 * TILE)[None] >> 5) < counts).astype(F32)
    *back, edge_field, edge_terms = pl.pallas_call(
        edge_kernel,
        out_shape=buffers + (shape(2, CD, TILE), shape(6, 2, FD, TILE)),
        in_specs=[SM] + [VM] * 17,
        out_specs=[VM] * 6,
        scratch_shapes=[
            pltpu.VMEM((10, 2, FD, TILE), F32),
            pltpu.VMEM((6 * FD, 2 * TILE), F32),
            pltpu.SMEM((40,), jnp.int32),
        ],
        compiler_params=params(),
        cost_estimate=cost(1_000_000_000, 3_000_000),
        name="edge_elements",
    )(faces, near, *ghosts, src, wide, alive, angles, *ops)
    returned = exchange(*back, False)
    field, total = pl.pallas_call(
        inner_kernel,
        out_shape=(shape(CD, 2, 2, TILE), shape(10, 2, FD, TILE)),
        in_specs=[SM] + [VM] * 16,
        out_specs=[VM] * 2,
        scratch_shapes=[
            pltpu.VMEM((6 * FD, 2 * TILE), F32),
            pltpu.VMEM((2, CD, TILE), F32),
            pltpu.VMEM((6, 2, FD, TILE), F32),
        ],
        compiler_params=params(),
        cost_estimate=cost(1_000_000_000, 3_000_000),
        name="inner_elements",
    )(faces, near, src, wide, alive, edge_field, edge_terms, ahead_field, ahead_terms, *ops)
    residual = pl.pallas_call(
        final_kernel,
        out_shape=linear,
        in_specs=[SM] + [VM] * 5,
        out_specs=VM,
        scratch_shapes=[pltpu.VMEM((6, 2, FD, TILE), F32)],
        compiler_params=params(),
        cost_estimate=cost(0, 1_000_000),
        name="final_sum",
    )(send_near, total, *returned)
    return parted(field), parted(residual)


def solution(mesh):
    spread = ("span", "chord")
    in_specs = (
        P(None, None, spread),
        P(None, None, spread),
        P(None, spread),
        P(),
        P(),
        P(),
        P(),
        P(spread, None),
        P("span", "chord", None, None),
        P("span", "chord"),
    )
    out_specs = (P(None, None, spread), P(None, None, spread))
    return jax.shard_map(local, mesh=mesh, in_specs=in_specs, out_specs=out_specs, check_vma=False)
```

```python
import math

import jax
import jax.numpy as jnp
from jax import lax
from jax.experimental import pallas as pl
from jax.experimental.pallas import tpu as pltpu
from jax.sharding import PartitionSpec as P

ANG = 32
EARLY = 0
FD = 45
CD = 135
TILE = 128
F32 = jnp.float32
BF16 = jnp.bfloat16

VM = pl.BlockSpec(memory_space=pltpu.VMEM)
SM = pl.BlockSpec(memory_space=pltpu.SMEM)
HB = pl.BlockSpec(memory_space=pltpu.HBM)


def place():
    s, c = lax.axis_index("span"), lax.axis_index("chord")
    return s, c, lax.axis_size("span")


def sides(s, c):
    odd_s, odd_c = s & 1, c & 1
    return 3 - odd_s, 2 + odd_s, 1 - odd_c, odd_c


def lane_group(rows):
    return lax.broadcasted_iota(jnp.int32, (rows, TILE), 1) >> 5


def shifted(block, source, target):
    return pltpu.roll(block, ((target - source) & 3) * ANG, 1)


def split(x):
    high = x.astype(BF16)
    return high, (x - high.astype(F32)).astype(BF16)


def mm(left, right):
    return jnp.dot(left, right, preferred_element_type=F32)


def triple(left, right):
    (lh, ll), (rh, rl) = left, right
    return mm(lh, rh) + (mm(lh, rl) + mm(ll, rh))


def complex_parts(real_rows, imag_rows):
    re = real_rows[:, :TILE] - imag_rows[:, TILE:]
    im = imag_rows[:, :TILE] + real_rows[:, TILE:]
    return re, im


def rows_of(ref, tile, part, tiles, count):
    return ref.reshape(count * tiles * 2, TILE), pl.ds(2 * tile + part, count, stride=2 * tiles)


def element_columns(first, faces, read, cols, src, scales, alive, ops, field, terms):
    half = first // 4
    group = lane_group(FD)
    for m in range(6):
        refs = [faces[first + k, m] for k in range(4)]
        for part in range(2):
            value = None
            for k, ref in enumerate(refs):
                moved = shifted(read(ref >> 2, part), ref & 3, k)
                value = moved if k == 0 else jnp.where(group == k, moved, value)
            cols[pl.ds(FD * m, FD), pl.ds(TILE * part, TILE)] = value
    x = split(cols[...])
    lh, ll, ih, il, th, tl, sh, sl = ops
    re, im = complex_parts(*[triple((lh[p], ll[p]), x) for p in range(2)])
    scale = scales[:, pl.ds(TILE * half, TILE)]
    rhs = split(jnp.concatenate([scale * (src[0, half] - re), scale * (src[1, half] - im)], axis=1))
    re, im = complex_parts(*[triple((ih[p], il[p]), rhs) for p in range(2)])
    alive = 1.0 if alive is None else alive[:, pl.ds(TILE * half, TILE)]
    re, im = re * alive, im * alive
    field[0], field[1] = re, im
    inner = split(jnp.concatenate([re, im], axis=1))
    out = [triple((th[p], tl[p]), inner) + triple((sh[p], sl[p]), x) for p in range(2)]
    for part, value in enumerate(complex_parts(*out)):
        value = value * alive
        for m in range(6):
            terms[m, part] = value[FD * m : FD * m + FD]


def turn(re, im, sign, angles):
    cosine = jnp.where(sign == 0, 1.0, angles[0:1, :])
    sine = sign.astype(F32) * angles[1:2, :]
    return re * cosine - im * sine, re * sine + im * cosine


def early(s):
    return ((s >> 1) & 3) <= EARLY


def pack_kernel(send_far, traces, faces_far, *rest):
    weights, (on_chip, span, even, odd, near, send_near, faces_near) = rest[:6], rest[6:13]
    ops, (src, wide, angles, field, terms) = rest[13:21], rest[21:26]
    held, (cols, plain, sems) = rest[26:32], rest[32:]
    s, c, _ = place()
    group = lane_group(FD)
    pairs = ((send_far, send_near), (traces, near), (faces_far, faces_near))
    pairs += tuple(zip(weights, held))
    copies = [pltpu.make_async_copy(a, b, sems.at[k]) for k, (a, b) in enumerate(pairs)]
    for copy in copies:
        copy.start()
    for copy in copies[:2]:
        copy.wait()

    def read(tile, part):
        flat, rows = rows_of(near, tile, part, 6, FD)
        return flat[rows, :]

    for side, out in zip(sides(s, c), (on_chip, span, even, odd)):
        numbers = [send_near[0, 0, side, j] for j in range(4)]
        for part in range(2):
            value = None
            for j, face in enumerate(numbers):
                moved = shifted(read(face >> 2, part), face & 3, j)
                value = moved if j == 0 else jnp.where(group == j, moved, value)
            out[part] = value
    for copy in copies[2:]:
        copy.wait()

    @pl.when(early(s))
    def _():
        prepare(held, ops, src, wide, angles, plain)
        element_columns(4, faces_near, read, cols, src, wide, None, ops, field, terms)


def prepare(held, ops, src, wide, angles, plain):
    turns = lax.broadcasted_iota(jnp.int32, (1, TILE), 1) & (ANG - 1)
    sigma = 2.0 * math.pi * turns.astype(F32) / ANG
    angles[0:1, :], angles[1:2, :] = jnp.cos(sigma), jnp.sin(sigma)
    for k, slot in enumerate(held[:4]):
        for part in range(2):
            rows, _, columns = slot.shape
            plain[pl.ds(0, rows), pl.ds(0, columns)] = slot[:, part, :]
            matrix = plain[pl.ds(0, rows), pl.ds(0, columns)]
            if k == 2:
                matrix = matrix.T
            ops[2 * k][part], ops[2 * k + 1][part] = split(matrix)
    for part in range(2):
        for half in range(2):
            flat, rows = rows_of(held[4], half, part, 2, CD)
            src[part, half] = flat[rows, :]
    column = lax.broadcasted_iota(jnp.int32, (CD, 2 * TILE), 1) >> 5
    tall = held[5][...].T
    value = None
    for e in range(8):
        spread = jnp.broadcast_to(tall[:, e : e + 1], (CD, 2 * TILE))
        value = spread if e == 0 else jnp.where(column == e, spread, value)
    wide[...] = value


def prepare_kernel(*refs):
    held, outs, plain = refs[:6], refs[17:28], refs[28]

    @pl.when(jnp.logical_not(early(place()[0])))
    def _():
        prepare(held, outs[:8], *outs[8:], plain)


def edge_kernel(faces, traces, span, odd, even, on_chip, src, scales, alive, angles, *rest):
    ops, (b_on, b_span, b_even, b_odd, field, terms, table, cols, where) = rest[:8], rest[8:]
    s, c, length = place()
    side = sides(s, c)
    sign = jnp.where(s == 0, -1, jnp.where(s == length - 1, 1, 0))
    for tile in range(6):
        for part in range(2):
            flat, rows = rows_of(traces, tile, part, 6, FD)
            table[tile, part] = flat[rows, :]
    for d, ref in zip((side[0], side[2], side[3]), (on_chip, even, odd)):
        for part in range(2):
            table[6 + d, part] = ref[part]
    table[6 + side[1], 0], table[6 + side[1], 1] = turn(span[0], span[1], sign, angles)
    for k in range(4):
        for m in range(6):
            where[faces[k, m]] = 4 * m + k
    element_columns(
        0, faces, lambda tile, part: table[tile, part], cols, src, scales, alive, ops, field, terms
    )
    group = lane_group(FD)
    for d, ref in zip(side, (b_on, b_span, b_even, b_odd)):
        spots = [where[24 + 4 * d + j] for j in range(4)]
        parts = []
        for part in range(2):
            value = None
            for j, spot in enumerate(spots):
                moved = shifted(terms[spot >> 2, part], spot & 3, j)
                value = moved if j == 0 else jnp.where(group == j, moved, value)
            parts.append(value)
        if ref is b_span:
            parts = turn(*parts, -sign, angles)
        ref[0], ref[1] = parts


def inner_kernel(faces, traces, src, scales, alive, edge_field, edge_terms, ahead_field, ahead_terms, *rest):
    ops, (field, sums, cols, inner, terms) = rest[:8], rest[8:]
    ahead = early(place()[0])

    def read(tile, part):
        flat, rows = rows_of(traces, tile, part, 6, FD)
        return flat[rows, :]

    @pl.when(ahead)
    def _():
        inner[...] = ahead_field[...]
        terms[...] = ahead_terms[...]

    @pl.when(jnp.logical_not(ahead))
    def _():
        element_columns(4, faces, read, cols, src, scales, None, ops, inner, terms)

    live = alive[:, pl.ds(TILE, TILE)]
    for part in range(2):
        inner[part] *= live
        for m in range(6):
            terms[m, part] *= live
        for half, values in enumerate((edge_field, inner)):
            flat, rows = rows_of(field, half, part, 2, CD)
            flat[rows, :] = values[part]
    sums[...] = jnp.zeros(sums.shape, F32)
    group = lane_group(FD)
    for source, first in ((edge_terms, 0), (terms, 4)):
        for m in range(6):
            for k in range(4):
                ref = faces[first + k, m]
                hit = group == (ref & 3)
                for part in range(2):
                    sums[ref >> 2, part] += jnp.where(hit, shifted(source[m, part], k, ref & 3), 0.0)


def final_kernel(send, total, span, even, odd, on_chip, out, sums, staged, sems):
    s, c, _ = place()
    sums[...] = total[pl.ds(0, 6)]
    group = lane_group(FD)
    for side, ref in zip(sides(s, c), (on_chip, span, even, odd)):
        for j in range(4):
            face = send[0, 0, side, j]
            hit = group == (face & 3)
            for part in range(2):
                sums[face >> 2, part] += jnp.where(hit, shifted(ref[part], j, face & 3), 0.0)
    copies = []
    for k, (first, count) in enumerate(((0, 24), (24, FD - 24))):
        for tile in range(6):
            for part in range(2):
                flat = staged.reshape(FD * 12, TILE)
                rows = pl.ds(12 * first + 2 * tile + part, count, stride=12)
                flat[rows, :] = sums[tile, part, pl.ds(first, count), :]
        rows = pl.ds(first, count)
        copies.append(pltpu.make_async_copy(staged.at[rows], out.at[rows], sems.at[k]))
        copies[k].start()
    for copy in copies:
        copy.wait()


def swaps(count, periodic):
    even = [(i, i ^ 1) for i in range(count)]
    odd = [pair for i in range(1, count - 1, 2) for pair in ((i, i + 1), (i + 1, i))]
    if periodic:
        odd += [(count - 1, 0), (0, count - 1)]
    return even, odd


def exchange(on_chip, span, even, odd, odd_first):
    span_even, span_odd = swaps(lax.axis_size("span"), True)
    chord_even, chord_odd = swaps(lax.axis_size("chord"), False)
    plan = [(even, "chord", chord_even), (odd, "chord", chord_odd)]
    if odd_first:
        plan.reverse()
    plan = [(span, "span", span_odd), *plan, (on_chip, "span", span_even)]
    return [lax.ppermute(*step) for step in plan]


def shape(*dims, dtype=F32):
    return jax.ShapeDtypeStruct(dims, dtype)


def params(**kwargs):
    return pltpu.CompilerParams(vmem_limit_bytes=32 * 1024 * 1024, **kwargs)


def cost(flops, size):
    return pl.CostEstimate(flops=flops, bytes_accessed=size, transcendentals=0)


def interleaved(array):
    _, rows, lanes = array.shape
    return array.transpose(1, 0, 2).reshape(rows, 2, lanes // TILE, TILE).transpose(0, 2, 1, 3)


def hbm(array):
    return pltpu.with_memory_space_constraint(array, pltpu.HBM)


def parted(array):
    rows, tiles = array.shape[:2]
    return array.transpose(0, 2, 1, 3).reshape(rows, 2, tiles * TILE).transpose(1, 0, 2)


def local(
    traces, source, scales, inverse_local, lift_map, trace_map, stabilizer, elem_faces, send_faces, counts
):
    buffers = (shape(2, FD, TILE),) * 4
    linear = shape(FD, 6, 2, TILE)

    weights = (
        lift_map.transpose(1, 0, 2),
        inverse_local.transpose(1, 0, 2),
        trace_map.transpose(2, 0, 1),
        stabilizer.transpose(1, 0, 2),
        interleaved(source),
        scales.T,
    )
    weights = tuple(map(hbm, weights))
    prepared = [
        shape(*w.shape, dtype=BF16)
        for w in (lift_map, inverse_local, trace_map, stabilizer)
        for _ in range(2)
    ] + [shape(2, 2, CD, TILE), shape(CD, 2 * TILE), shape(2, TILE)]
    held = [shape(*w.shape) for w in weights]
    plain = pltpu.VMEM(weights[3].shape[::2], F32)
    results = [shape(2, CD, TILE), shape(6, 2, FD, TILE)]
    numbers = [pltpu.SMEM(a.shape, jnp.int32) for a in (send_faces, elem_faces)]
    *packed, ahead_field, ahead_terms, k0, k1, k2, k3, k4, k5 = pl.pallas_call(
        pack_kernel,
        out_shape=[*buffers, linear, *numbers, *prepared, *results, *held],
        in_specs=[HB] * 9,
        out_specs=[VM] * 5 + [SM] * 2 + [VM] * 19,
        scratch_shapes=[
            pltpu.VMEM((6 * FD, 2 * TILE), F32),
            plain,
            pltpu.SemaphoreType.DMA((9,)),
        ],
        compiler_params=params(),
        cost_estimate=cost(0, 600_000),
        name="pack",
    )(hbm(send_faces), hbm(interleaved(traces)), hbm(elem_faces), *weights)
    sent, near, send_near, faces, ready = packed[:4], packed[4], packed[5], packed[6], packed[7:]
    ghosts = exchange(*sent, True)
    ready = pl.pallas_call(
        prepare_kernel,
        out_shape=prepared,
        in_specs=[VM] * 17,
        out_specs=[VM] * 11,
        input_output_aliases={6 + k: k for k in range(11)},
        scratch_shapes=[plain],
        compiler_params=params(),
        cost_estimate=cost(0, 3_000_000),
        name="prepare",
    )(k0, k1, k2, k3, k4, k5, *ready)
    ops, (src, wide, angles) = ready[:8], ready[8:]
    alive = ((jnp.arange(2 * TILE)[None] >> 5) < counts).astype(F32)
    *back, edge_field, edge_terms = pl.pallas_call(
        edge_kernel,
        out_shape=buffers + (shape(2, CD, TILE), shape(6, 2, FD, TILE)),
        in_specs=[SM] + [VM] * 17,
        out_specs=[VM] * 6,
        scratch_shapes=[
            pltpu.VMEM((10, 2, FD, TILE), F32),
            pltpu.VMEM((6 * FD, 2 * TILE), F32),
            pltpu.SMEM((40,), jnp.int32),
        ],
        compiler_params=params(),
        cost_estimate=cost(1_000_000_000, 3_000_000),
        name="edge_elements",
    )(faces, near, *ghosts, src, wide, alive, angles, *ops)
    returned = exchange(*back, False)
    field, total = pl.pallas_call(
        inner_kernel,
        out_shape=(shape(CD, 2, 2, TILE), shape(10, 2, FD, TILE)),
        in_specs=[SM] + [VM] * 16,
        out_specs=[VM] * 2,
        scratch_shapes=[
            pltpu.VMEM((6 * FD, 2 * TILE), F32),
            pltpu.VMEM((2, CD, TILE), F32),
            pltpu.VMEM((6, 2, FD, TILE), F32),
        ],
        compiler_params=params(),
        cost_estimate=cost(1_000_000_000, 3_000_000),
        name="inner_elements",
    )(faces, near, src, wide, alive, edge_field, edge_terms, ahead_field, ahead_terms, *ops)
    residual = pl.pallas_call(
        final_kernel,
        out_shape=linear,
        in_specs=[SM] + [VM] * 5,
        out_specs=HB,
        scratch_shapes=[
            pltpu.VMEM((6, 2, FD, TILE), F32),
            pltpu.VMEM((FD, 6, 2, TILE), F32),
            pltpu.SemaphoreType.DMA((2,)),
        ],
        compiler_params=params(),
        cost_estimate=cost(0, 1_000_000),
        name="final_sum",
    )(send_near, total, *returned)
    return parted(field), parted(residual)


def solution(mesh):
    spread = ("span", "chord")
    in_specs = (
        P(None, None, spread),
        P(None, None, spread),
        P(None, spread),
        P(),
        P(),
        P(),
        P(),
        P(spread, None),
        P("span", "chord", None, None),
        P("span", "chord"),
    )
    out_specs = (P(None, None, spread), P(None, None, spread))
    return jax.shard_map(local, mesh=mesh, in_specs=in_specs, out_specs=out_specs, check_vma=False)
```
